32 devices in a mesh: chan: 8 (over z, x), win: 4 (over y, core).
Axes of the slice: x: 2, y: 2, z: 4, core: 2. Of those that a mesh axis runs over, the one named last changes fastest.
Arguments:
- spectra: bfloat16 [8, 128, 128, 2, 128], P('chan', None, 'win'), may hold values from -6 to 6
- counts: int32 [128, 8], P('win'), may hold values from 1 to 256
- partner: int32 [2, 8], replicated, may hold values from 0 to 7, as said below
Outputs:
- cross: bfloat16 [8, 2, 128, 128, 256], P('win', None, 'chan')
The draws below stay inside these ranges and needn't reach their ends.
Inputs may be any that keep to these rules, and one draw needn't show every extreme that they name: Each row of partner is one cycle through all 8 blocks: a permutation with no block its own partner and no two blocks each other's partners.
All inputs are finite; a program needn't handle non-finite values.
Results may differ from the reference program's by a relative error of at most 0.015.
Values may be sent and summed in bfloat16 or wider, within the bound.
A program may use at most 128 MiB of HBM per device.

```python
import jax
import jax.numpy as jnp
from jax import lax

CB = 128
F = 128
W_DEV = 32
R = 2
NSAMP = 256
BLOCKS = 8
W_TOTAL = 128
N_WIN = 4


def draw_partner(key, part):
    rows = []
    for round_index in range(R):
        order = jax.random.permutation(jax.random.fold_in(key, round_index + 11), BLOCKS).astype(jnp.int32)
        following = jnp.roll(order, -1)
        row = jnp.zeros((BLOCKS,), jnp.int32).at[order].set(following)
        rows.append(row)
    return jnp.stack(rows)


def set_ends(drawn, rng, least, high):
    longest = drawn.shape.index(max(drawn.shape))
    spots = []
    for shift in (0, 1):
        where = [jax.random.randint(jax.random.fold_in(rng, axis), (), 0, length) for axis, length in enumerate(drawn.shape)]
        where[longest] = (where[longest] + shift) % drawn.shape[longest]
        spots.append(tuple(where))
    return drawn.at[spots[0]].set(least).at[spots[1]].set(high)


def levels(own_key, dims, shards, smallest, high):
    gain, own = 1.0, jax.random.fold_in(own_key, 6)
    for dim, blocks in shards:
        steps = jnp.exp(jax.random.uniform(jax.random.fold_in(own, dim), (blocks,), jnp.float32, smallest / len(shards), high / len(shards)))
        gain = gain * jnp.repeat(steps, dims[dim] // blocks).reshape([-1 if axis == dim else 1 for axis in range(len(dims))])
    return gain


def bell_draw(key, shape, spread, bound, shards=(), held_as=jnp.bfloat16):
    values = spread * jax.random.normal(key, shape, jnp.float32)
    if shards:
        values = values * levels(key, shape, shards, -0.22, 0.18)
    return jnp.clip(values, -bound, bound).astype(held_as)


def setup_inputs(seed: int = 0) -> dict:
    keys = jax.random.split(jax.random.key(seed), 4)
    return {
        "spectra": bell_draw(keys[0], (BLOCKS, F, W_TOTAL, 2, CB), 1.0, 6.0, ((0, 8), (2, 4))),
        "counts": set_ends(jax.random.randint(keys[1], (W_TOTAL, BLOCKS), 1, NSAMP + 1), jax.random.fold_in(keys[1], 1), 1, NSAMP).astype(jnp.int32),
        "partner": draw_partner(jax.random.fold_in(keys[3], 71), 0),
    }


EPS = 1e-06

def reference(spectra, counts, partner):
    values = spectra.astype(jnp.float32)
    power = lax.optimization_barrier(jnp.mean(lax.optimization_barrier(jnp.sum(values * values, axis=3)), axis=1))
    whitened = (values * lax.rsqrt(power + EPS)[:, None, :, None, :]).astype(jnp.bfloat16)
    blocks = whitened.reshape(BLOCKS, F, N_WIN, W_DEV, 2, CB)
    tallies = counts.astype(jnp.float32).T
    weight = jnp.minimum(tallies[None], jnp.take(tallies, partner, axis=0)) / NSAMP
    norm = jnp.sqrt(lax.optimization_barrier(jnp.sum(weight * weight, axis=2)))
    grouped = weight.reshape(R, BLOCKS, N_WIN, W_DEV)

    def one_block(index):
        own = lax.dynamic_index_in_dim(blocks, index, 0, keepdims=False)
        mates = jnp.take(blocks, partner[:, index], axis=0)
        scale = grouped[:, index]
        weighted = (scale[:, None, :, :, None, None] * own[None].astype(jnp.float32)).astype(jnp.bfloat16)
        rotated = jnp.stack([-mates[..., 1, :], mates[..., 0, :]], axis=-2)
        paired = jnp.stack([mates, rotated], axis=-2)
        partial_value = jnp.einsum('rfgwkc,rfgwkod->grfcod', weighted.astype(jnp.float32), paired.astype(jnp.float32))
        partial_value = lax.optimization_barrier(partial_value.astype(jnp.bfloat16))
        total = lax.optimization_barrier(jnp.sum(partial_value.astype(jnp.float32), axis=0))
        result = total / norm[:, index][:, None, None, None, None]
        return result.astype(jnp.bfloat16).reshape(R, F, CB, 2 * CB)
    return lax.map(one_block, jnp.arange(BLOCKS))
```

```python
import functools

import jax
import jax.numpy as jnp
from jax import lax
from jax.experimental import pallas as pl
from jax.experimental.pallas import tpu as pltpu
from jax.sharding import PartitionSpec as P

NSAMP = 256
EPS = 1e-06
LANES = 128
MESH = pl.DeviceIdType.MESH


def flip(index, bits):
    out, place = index, 1
    while place <= bits:
        if bits & place:
            out = out + place * (1 - 2 * ((index // place) % 2))
        place *= 2
    return out


def kernel(cfg, x_ref, counts_ref, partner_ref, out_ref, *scratch):
    nchan, groups, nsub, per_sub, chosen, rounds, windows, width = cfg
    (send, tall, raw, wgt, inv, stage, sem_as, sem_ar, sem_ys, sem_yr, sem_bs, sem_br,
     sem_cs, sem_cr, sem_ts, sem_tr, sem_out) = scratch[:17]
    held = scratch[17:]
    bins = nsub * per_sub
    total_bins = nchan * bins
    me = lax.axis_index("chan")
    mine = lax.axis_index("win")
    across, beside = flip(mine, 2), flip(mine, 1)
    rows = 2 * windows

    barrier = pltpu.get_barrier_semaphore()
    for d in range(1, nchan):
        pl.semaphore_signal(barrier, 1, device_id={"chan": flip(me, d)}, device_id_type=MESH)
    for d in range(1, groups):
        pl.semaphore_signal(barrier, 1, device_id={"win": flip(mine, d)}, device_id_type=MESH)

    def to_bins(s, d):
        return pltpu.make_async_remote_copy(
            src_ref=send.at[s, flip(me, d)], dst_ref=held[s].at[me, mine],
            send_sem=sem_as.at[s, d], recv_sem=sem_ar.at[s, d],
            device_id={"chan": flip(me, d)}, device_id_type=MESH)

    def to_across(s, d):
        block = held[s].at[flip(me, d), mine]
        return pltpu.make_async_remote_copy(
            src_ref=block, dst_ref=block, send_sem=sem_ys.at[s, d], recv_sem=sem_yr.at[s, d],
            device_id={"win": across}, device_id_type=MESH)

    def to_beside(s, d):
        block = held[s].at[flip(me, d), mine]
        return pltpu.make_async_remote_copy(
            src_ref=block, dst_ref=block, send_sem=sem_bs.at[s, d], recv_sem=sem_br.at[s, d],
            device_id={"win": beside}, device_id_type=MESH)

    def relay(s, d):
        block = held[s].at[flip(me, d), across]
        return pltpu.make_async_remote_copy(
            src_ref=block, dst_ref=block, send_sem=sem_cs.at[s, d], recv_sem=sem_cr.at[s, d],
            device_id={"win": beside}, device_id_type=MESH)

    def tallies(d):
        return pltpu.make_async_remote_copy(
            src_ref=tall.at[mine], dst_ref=tall.at[mine],
            send_sem=sem_ts.at[d], recv_sem=sem_tr.at[d],
            device_id={"win": flip(mine, d)}, device_id_type=MESH)

    def store_out(s):
        return pltpu.make_async_copy(
            stage.at[s], out_ref.at[:, :, pl.ds(s * per_sub, per_sub)], sem_out.at[s])

    def add_power(f, acc):
        v = x_ref[f].astype(jnp.float32)
        return acc + v * v

    acc = lax.fori_loop(0, total_bins, add_power, jnp.zeros((rows, width), jnp.float32), unroll=4)
    raw[0] = acc
    power = (raw[0, pl.ds(0, windows, stride=2), :] + raw[0, pl.ds(1, windows, stride=2), :]) * (1.0 / total_bins)
    scale = lax.rsqrt(power + EPS)

    def whiten(s):
        def one(j, carry):
            for q in range(per_sub):
                raw[q] = x_ref[j * bins + s * per_sub + q].astype(jnp.float32)
            for q in range(per_sub):
                for k in range(2):
                    part = raw[q, pl.ds(k, windows, stride=2), :] * scale
                    send[s, j, q, pl.ds(k * windows, windows), :] = part.astype(jnp.bfloat16)
            return carry

        lax.fori_loop(0, nchan, one, 0)
        held[s][me, mine] = send[s, me]

    tall[mine] = jnp.zeros((windows, LANES), jnp.float32)
    tall[mine, :, pl.ds(0, counts_ref.shape[1])] = counts_ref[...].astype(jnp.float32)

    whiten(0)
    pl.semaphore_wait(barrier, nchan - 1 + groups - 1)
    for d in range(nchan - 1, 0, -1):
        to_bins(0, d).start()
    for d in range(1, groups):
        tallies(d).start()
    for s in range(1, nsub):
        whiten(s)
        if s < AHEAD:
            for d in range(nchan - 1, 0, -1):
                to_bins(s, d).start()

    def weights():
        for d in range(1, groups):
            tallies(d).wait_recv()
        c = tall[...].reshape(groups * windows, LANES)
        lane = lax.broadcasted_iota(jnp.int32, c.shape, 1)
        first = mine * chosen

        def column(a):
            return jnp.sum(jnp.where(lane == a, c, 0.0), axis=1, keepdims=True)

        def one(n, carry):
            own = column(first + n)
            for r in range(rounds):
                w = jnp.minimum(own, column(partner_ref[r, first + n])) * (1.0 / NSAMP)
                w = jnp.broadcast_to(w, (groups * windows, width))
                wgt[n, r] = w.astype(jnp.bfloat16)
                norm = lax.rsqrt(jnp.sum(w * w, axis=0, keepdims=True))
                inv[n, r] = jnp.broadcast_to(norm, (8, width))
            return carry

        lax.fori_loop(0, chosen, one, 0)

    def planes(s, block, q):
        return [
            jnp.concatenate(
                [held[s][block, g, q, pl.ds(k * windows, windows), :] for g in range(groups)], axis=0)
            for k in range(2)
        ]

    def unit(s, u):
        n, q = u // per_sub, u % per_sub
        a = mine * chosen + n
        re, im = planes(s, a, q)
        re, im = re.T, im.T
        lhs = jnp.concatenate(
            [jnp.concatenate([re, im], axis=1), jnp.concatenate([im, -re], axis=1)], axis=0)
        mates = []
        for r in range(rounds):
            w = wgt[n, r]
            mre, mim = planes(s, partner_ref[r, a], q)
            mates.append(jnp.concatenate([mre * w, mim * w], axis=0))
        rhs = jnp.concatenate(mates, axis=1)
        res = jnp.dot(lhs, rhs, preferred_element_type=jnp.float32)
        for r in range(rounds):
            norm = inv[n, r, pl.ds(0, 1), :]
            for k in range(2):
                tile = res[k * width:(k + 1) * width, r * width:(r + 1) * width] * norm
                stage[s, n, r, q, :, pl.ds(k * width, width)] = tile.astype(jnp.bfloat16)

    units = chosen * per_sub

    def compute(s, low, high):
        lax.fori_loop(low, high, lambda u, carry: (unit(s, u), carry)[1], 0)

    def settle(s):
        for d in range(nchan):
            to_beside(s, d).wait_recv()
            relay(s, d).wait_recv()

    late = nchan // 2
    previous = None
    for s in range(nsub):
        for d in range(nchan):
            if d:
                to_bins(s, d).wait_recv()
            to_across(s, d).start()
            to_beside(s, d).start()
            if d and s + AHEAD < nsub:
                to_bins(s + AHEAD, nchan - d).start()
            if previous is not None:
                to_across(*previous).wait_recv()
                relay(*previous).start()
            previous = (s, d)
            if s == 0 and d == nchan - 1:
                weights()
            if s and d >= late:
                if d == late:
                    settle(s - 1)
                step = d - late
                compute(s - 1, step * units // (nchan - late), (step + 1) * units // (nchan - late))
        if s:
            store_out(s - 1).start()
    to_across(*previous).wait_recv()
    relay(*previous).start()
    settle(nsub - 1)
    compute(nsub - 1, 0, units)
    store_out(nsub - 1).start()

    for d in range(1, groups):
        tallies(d).wait_send()
    for s in range(nsub):
        for d in range(nchan):
            if d:
                to_bins(s, d).wait_send()
            to_across(s, d).wait_send()
            to_beside(s, d).wait_send()
            relay(s, d).wait_send()
    for s in range(nsub):
        store_out(s).wait()


AHEAD = 2


def per_device(nchan, groups, spectra, counts, partner):
    _, total_bins, windows, parts, width = spectra.shape
    rounds, nblocks = partner.shape
    bins = total_bins // nchan
    chosen = nblocks // groups
    nsub = 4 if bins % 4 == 0 else bins
    per_sub = bins // nsub
    cfg = (nchan, groups, nsub, per_sub, chosen, rounds, windows, width)
    x = spectra.reshape(total_bins, windows * parts, width)
    dma = pltpu.SemaphoreType.DMA
    flops = 2 * chosen * rounds * bins * width * (2 * width) * (2 * groups * windows)
    return pl.pallas_call(
        functools.partial(kernel, cfg),
        out_shape=jax.ShapeDtypeStruct((chosen, rounds, bins, width, 2 * width), jnp.bfloat16),
        in_specs=[
            pl.BlockSpec(memory_space=pltpu.VMEM),
            pl.BlockSpec(memory_space=pltpu.VMEM),
            pl.BlockSpec(memory_space=pltpu.SMEM),
        ],
        out_specs=pl.BlockSpec(memory_space=pl.ANY),
        scratch_shapes=[
            pltpu.VMEM((nsub, nchan, per_sub, 2 * windows, width), jnp.bfloat16),
            pltpu.VMEM((groups, windows, LANES), jnp.float32),
            pltpu.VMEM((per_sub, 2 * windows, width), jnp.float32),
            pltpu.VMEM((chosen, rounds, groups * windows, width), jnp.bfloat16),
            pltpu.VMEM((chosen, rounds, 8, width), jnp.float32),
            pltpu.VMEM((nsub, chosen, rounds, per_sub, width, 2 * width), jnp.bfloat16),
        ]
        + [dma((nsub, nchan))] * 8
        + [dma((groups,))] * 2
        + [dma((nsub,))]
        + [pltpu.VMEM((nblocks, groups, per_sub, 2 * windows, width), jnp.bfloat16)] * nsub,
        compiler_params=pltpu.CompilerParams(
            collective_id=0, has_side_effects=True, vmem_limit_bytes=48 * 1024 * 1024),
        cost_estimate=pl.CostEstimate(flops=flops, bytes_accessed=8 << 20, transcendentals=0),
    )(x, counts, partner)


def solution(mesh):
    sizes = dict(mesh.shape)
    placed = (P("chan", None, "win", None, None), P("win", None), P())
    return jax.shard_map(
        functools.partial(per_device, sizes["chan"], sizes["win"]),
        mesh=mesh,
        in_specs=placed,
        out_specs=P("win", None, "chan", None, None),
        check_vma=False,
    )
```

```python
import functools

import jax
import jax.numpy as jnp
from jax import lax
from jax.experimental import pallas as pl
from jax.experimental.pallas import tpu as pltpu
from jax.sharding import PartitionSpec as P

NSAMP = 256
EPS = 1e-06
LANES = 128
AHEAD = 2
MESH = pl.DeviceIdType.MESH


def flip(index, bits):
    out, place = index, 1
    while place <= bits:
        if bits & place:
            out = out + place * (1 - 2 * ((index // place) % 2))
        place *= 2
    return out


def kernel(cfg, x_ref, counts_ref, partner_ref, out_ref, *scratch):
    nchan, groups, nsub, per_sub, chosen, rounds, windows, width = cfg
    (send, tall, raw, cts, wgt, inv, sem_as, sem_ar, sem_ys, sem_yr, sem_bs, sem_br,
     sem_cs, sem_cr, sem_ts, sem_tr) = scratch[:16]
    held = scratch[16:]
    bins = nsub * per_sub
    total_bins = nchan * bins
    me = lax.axis_index("chan")
    mine = lax.axis_index("win")
    across, beside = flip(mine, 2), flip(mine, 1)
    rows = 2 * windows

    barrier = pltpu.get_barrier_semaphore()
    for d in range(1, nchan):
        pl.semaphore_signal(barrier, 1, device_id={"chan": flip(me, d)}, device_id_type=MESH)
    for d in range(1, groups):
        pl.semaphore_signal(barrier, 1, device_id={"win": flip(mine, d)}, device_id_type=MESH)

    def to_bins(s, d):
        return pltpu.make_async_remote_copy(
            src_ref=send.at[s, flip(me, d)], dst_ref=held[s].at[me, mine],
            send_sem=sem_as.at[s, d], recv_sem=sem_ar.at[s, d],
            device_id={"chan": flip(me, d)}, device_id_type=MESH)

    def to_across(s, d):
        block = held[s].at[flip(me, d), mine]
        return pltpu.make_async_remote_copy(
            src_ref=block, dst_ref=block, send_sem=sem_ys.at[s, d], recv_sem=sem_yr.at[s, d],
            device_id={"win": across}, device_id_type=MESH)

    def to_beside(s, d):
        block = held[s].at[flip(me, d), mine]
        return pltpu.make_async_remote_copy(
            src_ref=block, dst_ref=block, send_sem=sem_bs.at[s, d], recv_sem=sem_br.at[s, d],
            device_id={"win": beside}, device_id_type=MESH)

    def relay(s, d):
        block = held[s].at[flip(me, d), across]
        return pltpu.make_async_remote_copy(
            src_ref=block, dst_ref=block, send_sem=sem_cs.at[s, d], recv_sem=sem_cr.at[s, d],
            device_id={"win": beside}, device_id_type=MESH)

    def tallies(d):
        return pltpu.make_async_remote_copy(
            src_ref=tall.at[mine], dst_ref=tall.at[mine],
            send_sem=sem_ts.at[d], recv_sem=sem_tr.at[d],
            device_id={"win": flip(mine, d)}, device_id_type=MESH)

    def add_power(f, acc):
        v = x_ref[f].astype(jnp.float32)
        return acc + v * v

    acc = lax.fori_loop(0, total_bins, add_power, jnp.zeros((rows, width), jnp.float32), unroll=4)
    raw[0] = acc
    power = (raw[0, pl.ds(0, windows, stride=2), :] + raw[0, pl.ds(1, windows, stride=2), :]) * (1.0 / total_bins)
    scale = lax.rsqrt(power + EPS)

    def whiten(s):
        def one(j, carry):
            for q in range(per_sub):
                raw[q] = x_ref[j * bins + s * per_sub + q].astype(jnp.float32)
            for q in range(per_sub):
                for k in range(2):
                    part = raw[q, pl.ds(k, windows, stride=2), :] * scale
                    send[s, j, q, pl.ds(k * windows, windows), :] = part.astype(jnp.bfloat16)
            return carry

        lax.fori_loop(0, nchan, one, 0)
        held[s][me, mine] = send[s, me]

    tall[mine] = jnp.zeros(tall.shape[1:], jnp.float32)
    tall[mine, :, pl.ds(0, windows)] = counts_ref[...].astype(jnp.float32)

    whiten(0)
    pl.semaphore_wait(barrier, nchan - 1 + groups - 1)
    to_across(0, 0).start()
    to_beside(0, 0).start()
    for d in range(nchan - 1, 0, -1):
        to_bins(0, d).start()
    for d in range(1, groups):
        tallies(d).start()
    for s in range(1, AHEAD):
        whiten(s)
        for d in range(nchan - 1, 0, -1):
            to_bins(s, d).start()

    def weights():
        for d in range(1, groups):
            tallies(d).wait_recv()
        whole = tall[0]
        for g in range(1, groups):
            whole = whole + pltpu.roll(tall[g], g * windows, 1)
        cts[...] = whole
        first = mine * chosen

        def one(n, carry):
            own = cts[pl.ds(first + n, 1), :]
            for r in range(rounds):
                row = jnp.minimum(own, cts[pl.ds(partner_ref[r, first + n], 1), :]) * (1.0 / NSAMP)
                wgt[n, r] = jnp.broadcast_to(row, (LANES, LANES)).T.astype(jnp.bfloat16)
                norm = lax.rsqrt(jnp.sum(row * row, axis=1, keepdims=True))
                inv[n, r] = jnp.broadcast_to(norm, (8, width))
            return carry

        lax.fori_loop(0, chosen, one, 0)

    def planes(s, block, q):
        return [
            jnp.concatenate(
                [held[s][block, g, q, pl.ds(k * windows, windows), :] for g in range(groups)], axis=0)
            for k in range(2)
        ]

    def unit(s, u):
        n, q = u // per_sub, u % per_sub
        a = mine * chosen + n
        re, im = planes(s, a, q)
        re, im = re.T, im.T
        lhs = jnp.concatenate(
            [jnp.concatenate([re, im], axis=1), jnp.concatenate([im, -re], axis=1)], axis=0)
        mates = []
        for r in range(rounds):
            w = wgt[n, r]
            mre, mim = planes(s, partner_ref[r, a], q)
            mates.append(jnp.concatenate([mre * w, mim * w], axis=0))
        rhs = jnp.concatenate(mates, axis=1)
        res = jnp.dot(lhs, rhs, preferred_element_type=jnp.float32)
        for r in range(rounds):
            norm = inv[n, r, pl.ds(0, 1), :]
            for k in range(2):
                tile = res[k * width:(k + 1) * width, r * width:(r + 1) * width] * norm
                out_ref[n, r, s * per_sub + q, :, pl.ds(k * width, width)] = tile.astype(jnp.bfloat16)

    units = chosen * per_sub

    def compute(s, low, high):
        lax.fori_loop(low, high, lambda u, carry: (unit(s, u), carry)[1], 0, unroll=2 if (high - low) % 2 == 0 else 1)

    def settle(s):
        for d in range(nchan):
            to_beside(s, d).wait_recv()
            relay(s, d).wait_recv()

    def pass_on(step):
        s, d = step // nchan, step % nchan
        to_across(s, d).wait_recv()
        relay(s, d).start()

    lag = nchan // 2
    late = 5 * nchan // 8
    for s in range(nsub):
        for d in range(nchan):
            step = s * nchan + d
            if d:
                to_bins(s, d).wait_recv()
            if step:
                to_across(s, d).start()
                to_beside(s, d).start()
            if d == 0 and s + AHEAD < nsub:
                whiten(s + AHEAD)
            if d and s + AHEAD < nsub:
                to_bins(s + AHEAD, nchan - d).start()
            if step >= lag:
                pass_on(step - lag)
            if step == nchan - 1:
                weights()
            if s and d >= late:
                if d == late:
                    settle(s - 1)
                i = d - late
                compute(s - 1, i * units // (nchan - late), (i + 1) * units // (nchan - late))
    for step in range(nsub * nchan - lag, nsub * nchan):
        pass_on(step)
    settle(nsub - 1)
    compute(nsub - 1, 0, units)

    for d in range(1, groups):
        tallies(d).wait_send()
    for s in range(nsub):
        for d in range(nchan):
            if d:
                to_bins(s, d).wait_send()
            to_across(s, d).wait_send()
            to_beside(s, d).wait_send()
            relay(s, d).wait_send()


def per_device(nchan, groups, spectra, counts, partner):
    _, total_bins, windows, parts, width = spectra.shape
    rounds, nblocks = partner.shape
    bins = total_bins // nchan
    chosen = nblocks // groups
    nsub = 4 if bins % 4 == 0 else bins
    per_sub = bins // nsub
    cfg = (nchan, groups, nsub, per_sub, chosen, rounds, windows, width)
    x = spectra.reshape(total_bins, windows * parts, width)
    dma = pltpu.SemaphoreType.DMA
    flops = 2 * chosen * rounds * bins * width * (2 * width) * (2 * groups * windows)
    return pl.pallas_call(
        functools.partial(kernel, cfg),
        out_shape=jax.ShapeDtypeStruct((chosen, rounds, bins, width, 2 * width), jnp.bfloat16),
        in_specs=[
            pl.BlockSpec(memory_space=pltpu.VMEM),
            pl.BlockSpec(memory_space=pltpu.VMEM),
            pl.BlockSpec(memory_space=pltpu.SMEM),
        ],
        out_specs=pl.BlockSpec(memory_space=pltpu.VMEM),
        scratch_shapes=[
            pltpu.VMEM((nsub, nchan, per_sub, 2 * windows, width), jnp.bfloat16),
            pltpu.VMEM((groups, nblocks, LANES), jnp.float32),
            pltpu.VMEM((per_sub, 2 * windows, width), jnp.float32),
            pltpu.VMEM((nblocks, LANES), jnp.float32),
            pltpu.VMEM((chosen, rounds, groups * windows, width), jnp.bfloat16),
            pltpu.VMEM((chosen, rounds, 8, width), jnp.float32),
        ]
        + [dma((nsub, nchan))] * 8
        + [dma((groups,))] * 2
        + [pltpu.VMEM((nblocks, groups, per_sub, 2 * windows, width), jnp.bfloat16)] * nsub,
        compiler_params=pltpu.CompilerParams(
            collective_id=0, has_side_effects=True, vmem_limit_bytes=40 * 1024 * 1024),
        cost_estimate=pl.CostEstimate(flops=flops, bytes_accessed=8 << 20, transcendentals=0),
    )(x, counts.T, partner)


def solution(mesh):
    sizes = dict(mesh.shape)
    placed = (P("chan", None, "win", None, None), P("win", None), P())
    return jax.shard_map(
        functools.partial(per_device, sizes["chan"], sizes["win"]),
        mesh=mesh,
        in_specs=placed,
        out_specs=P("win", None, "chan", None, None),
        check_vma=False,
    )
```

```python
import functools

import jax
import jax.numpy as jnp
from jax import lax
from jax.experimental import pallas as pl
from jax.experimental.pallas import tpu as pltpu
from jax.sharding import PartitionSpec as P

NSAMP = 256
EPS = 1e-06
LANES = 128
AHEAD = 2
MESH = pl.DeviceIdType.MESH


def flip(index, bits):
    out, place = index, 1
    while place <= bits:
        if bits & place:
            out = out + place * (1 - 2 * ((index // place) % 2))
        place *= 2
    return out


def kernel(cfg, x_ref, counts_ref, partner_ref, out_ref, *scratch):
    nchan, groups, sizes, chosen, rounds, windows, width = cfg
    (tall, raw, cts, wgt, inv, sem_as, sem_ar, sem_ys, sem_yr, sem_bs, sem_br,
     sem_cs, sem_cr, sem_ts, sem_tr) = scratch[:15]
    nsub, bins = len(sizes), sum(sizes)
    starts = [sum(sizes[:s]) for s in range(nsub)]
    held, send = scratch[15:15 + nsub], scratch[15 + nsub:]
    total_bins = nchan * bins
    me = lax.axis_index("chan")
    mine = lax.axis_index("win")
    across, beside = flip(mine, 2), flip(mine, 1)
    rows = 2 * windows

    barrier = pltpu.get_barrier_semaphore()
    for d in range(1, nchan):
        pl.semaphore_signal(barrier, 1, device_id={"chan": flip(me, d)}, device_id_type=MESH)
    for d in range(1, groups):
        pl.semaphore_signal(barrier, 1, device_id={"win": flip(mine, d)}, device_id_type=MESH)

    def to_bins(s, d):
        return pltpu.make_async_remote_copy(
            src_ref=send[s].at[flip(me, d)], dst_ref=held[s].at[me, mine],
            send_sem=sem_as.at[s, d], recv_sem=sem_ar.at[s, d],
            device_id={"chan": flip(me, d)}, device_id_type=MESH)

    def to_across(s, d):
        block = held[s].at[flip(me, d), mine]
        return pltpu.make_async_remote_copy(
            src_ref=block, dst_ref=block, send_sem=sem_ys.at[s, d], recv_sem=sem_yr.at[s, d],
            device_id={"win": across}, device_id_type=MESH)

    def to_beside(s, d):
        block = held[s].at[flip(me, d), mine]
        return pltpu.make_async_remote_copy(
            src_ref=block, dst_ref=block, send_sem=sem_bs.at[s, d], recv_sem=sem_br.at[s, d],
            device_id={"win": beside}, device_id_type=MESH)

    def relay(s, d):
        block = held[s].at[flip(me, d), across]
        return pltpu.make_async_remote_copy(
            src_ref=block, dst_ref=block, send_sem=sem_cs.at[s, d], recv_sem=sem_cr.at[s, d],
            device_id={"win": beside}, device_id_type=MESH)

    def tallies(d):
        return pltpu.make_async_remote_copy(
            src_ref=tall.at[mine], dst_ref=tall.at[mine],
            send_sem=sem_ts.at[d], recv_sem=sem_tr.at[d],
            device_id={"win": flip(mine, d)}, device_id_type=MESH)

    def add_power(f, acc):
        v = x_ref[f].astype(jnp.float32)
        return acc + v * v

    acc = lax.fori_loop(0, total_bins, add_power, jnp.zeros((rows, width), jnp.float32), unroll=4)
    raw[0] = acc
    power = (raw[0, pl.ds(0, windows, stride=2), :] + raw[0, pl.ds(1, windows, stride=2), :]) * (1.0 / total_bins)
    scale = lax.rsqrt(power + EPS)

    def whiten(s):
        def one(j, carry):
            for q in range(sizes[s]):
                raw[q] = x_ref[j * bins + starts[s] + q].astype(jnp.float32)
            for q in range(sizes[s]):
                for k in range(2):
                    part = raw[q, pl.ds(k, windows, stride=2), :] * scale
                    send[s][j, q, pl.ds(k * windows, windows), :] = part.astype(jnp.bfloat16)
            return carry

        lax.fori_loop(0, nchan, one, 0)
        held[s][me, mine] = send[s][me]

    tall[mine] = jnp.zeros(tall.shape[1:], jnp.float32)
    tall[mine, :, pl.ds(0, windows)] = counts_ref[...].astype(jnp.float32)

    whiten(0)
    pl.semaphore_wait(barrier, nchan - 1 + groups - 1)
    to_across(0, 0).start()
    to_beside(0, 0).start()
    for d in range(nchan - 1, 0, -1):
        to_bins(0, d).start()
    for d in range(1, groups):
        tallies(d).start()
    for s in range(1, AHEAD):
        whiten(s)
        for d in range(nchan - 1, 0, -1):
            to_bins(s, d).start()

    def weights():
        for d in range(1, groups):
            tallies(d).wait_recv()
        whole = tall[0]
        for g in range(1, groups):
            whole = whole + pltpu.roll(tall[g], g * windows, 1)
        cts[...] = whole
        first = mine * chosen

        def one(n, carry):
            own = cts[pl.ds(first + n, 1), :]
            for r in range(rounds):
                row = jnp.minimum(own, cts[pl.ds(partner_ref[r, first + n], 1), :]) * (1.0 / NSAMP)
                wgt[n, r] = jnp.broadcast_to(row, (LANES, LANES)).T.astype(jnp.bfloat16)
                norm = lax.rsqrt(jnp.sum(row * row, axis=1, keepdims=True))
                inv[n, r] = jnp.broadcast_to(norm, (8, width))
            return carry

        lax.fori_loop(0, chosen, one, 0)

    def planes(s, block, q):
        return [
            jnp.concatenate(
                [held[s][block, g, q, pl.ds(k * windows, windows), :] for g in range(groups)], axis=0)
            for k in range(2)
        ]

    def unit(s, u):
        n, q = u // sizes[s], u % sizes[s]
        a = mine * chosen + n
        re, im = planes(s, a, q)
        re, im = re.T, im.T
        lhs = jnp.concatenate(
            [jnp.concatenate([re, im], axis=1), jnp.concatenate([im, -re], axis=1)], axis=0)
        mates = []
        for r in range(rounds):
            w = wgt[n, r]
            mre, mim = planes(s, partner_ref[r, a], q)
            mates.append(jnp.concatenate([mre * w, mim * w], axis=0))
        rhs = jnp.concatenate(mates, axis=1)
        res = jnp.dot(lhs, rhs, preferred_element_type=jnp.float32)
        for r in range(rounds):
            norm = inv[n, r, pl.ds(0, 1), :]
            for k in range(2):
                tile = res[k * width:(k + 1) * width, r * width:(r + 1) * width] * norm
                out_ref[n, r, starts[s] + q, :, pl.ds(k * width, width)] = tile.astype(jnp.bfloat16)

    def compute(s, low, high):
        lax.fori_loop(low, high, lambda u, carry: (unit(s, u), carry)[1], 0, unroll=2 if (high - low) % 2 == 0 else 1)

    def settle(s):
        for d in range(nchan):
            to_beside(s, d).wait_recv()
            relay(s, d).wait_recv()

    def pass_on(step):
        s, d = step // nchan, step % nchan
        to_across(s, d).wait_recv()
        relay(s, d).start()

    lag = nchan // 2
    late = 5 * nchan // 8
    for s in range(nsub):
        units = chosen * sizes[s - 1]
        for d in range(nchan):
            step = s * nchan + d
            if d:
                to_bins(s, d).wait_recv()
            if step:
                to_across(s, d).start()
                to_beside(s, d).start()
            if s == 0 and d % 2 == 0 and AHEAD + d // 2 < nsub:
                whiten(AHEAD + d // 2)
                for e in range(nchan - 1, 0, -1):
                    to_bins(AHEAD + d // 2, e).start()
            if step >= lag:
                pass_on(step - lag)
            if step == nchan - 1:
                weights()
            if s and d >= late:
                if d == late:
                    settle(s - 1)
                i = d - late
                compute(s - 1, i * units // (nchan - late), (i + 1) * units // (nchan - late))
    for step in range(nsub * nchan - lag, nsub * nchan):
        pass_on(step)
    settle(nsub - 1)
    compute(nsub - 1, 0, chosen * sizes[-1])

    for d in range(1, groups):
        tallies(d).wait_send()
    for s in range(nsub):
        for d in range(nchan):
            if d:
                to_bins(s, d).wait_send()
            to_across(s, d).wait_send()
            to_beside(s, d).wait_send()
            relay(s, d).wait_send()


def per_device(nchan, groups, spectra, counts, partner):
    _, total_bins, windows, parts, width = spectra.shape
    rounds, nblocks = partner.shape
    bins = total_bins // nchan
    chosen = nblocks // groups
    sizes = (bins // 4,) * 3 + (bins // 8,) * 2 if bins % 8 == 0 else (1,) * bins
    nsub = len(sizes)
    cfg = (nchan, groups, sizes, chosen, rounds, windows, width)
    x = spectra.reshape(total_bins, windows * parts, width)
    dma = pltpu.SemaphoreType.DMA
    flops = 2 * chosen * rounds * bins * width * (2 * width) * (2 * groups * windows)
    return pl.pallas_call(
        functools.partial(kernel, cfg),
        out_shape=jax.ShapeDtypeStruct((chosen, rounds, bins, width, 2 * width), jnp.bfloat16),
        in_specs=[
            pl.BlockSpec(memory_space=pltpu.VMEM),
            pl.BlockSpec(memory_space=pltpu.VMEM),
            pl.BlockSpec(memory_space=pltpu.SMEM),
        ],
        out_specs=pl.BlockSpec(memory_space=pltpu.VMEM),
        scratch_shapes=[
            pltpu.VMEM((groups, nblocks, LANES), jnp.float32),
            pltpu.VMEM((max(sizes), 2 * windows, width), jnp.float32),
            pltpu.VMEM((nblocks, LANES), jnp.float32),
            pltpu.VMEM((chosen, rounds, groups * windows, width), jnp.bfloat16),
            pltpu.VMEM((chosen, rounds, 8, width), jnp.float32),
        ]
        + [dma((nsub, nchan))] * 8
        + [dma((groups,))] * 2
        + [pltpu.VMEM((nblocks, groups, size, 2 * windows, width), jnp.bfloat16) for size in sizes]
        + [pltpu.VMEM((nchan, size, 2 * windows, width), jnp.bfloat16) for size in sizes],
        compiler_params=pltpu.CompilerParams(
            collective_id=0, has_side_effects=True, vmem_limit_bytes=40 * 1024 * 1024),
        cost_estimate=pl.CostEstimate(flops=flops, bytes_accessed=8 << 20, transcendentals=0),
    )(x, counts.T, partner)


def solution(mesh):
    sizes = dict(mesh.shape)
    placed = (P("chan", None, "win", None, None), P("win", None), P())
    return jax.shard_map(
        functools.partial(per_device, sizes["chan"], sizes["win"]),
        mesh=mesh,
        in_specs=placed,
        out_specs=P("win", None, "chan", None, None),
        check_vma=False,
    )
```

```python
import functools

import jax
import jax.numpy as jnp
from jax import lax
from jax.experimental import pallas as pl
from jax.experimental.pallas import tpu as pltpu
from jax.sharding import PartitionSpec as P

NSAMP = 256
EPS = 1e-06
LANES = 128
AHEAD = 2
MESH = pl.DeviceIdType.MESH


def flip(index, bits):
    out, place = index, 1
    while place <= bits:
        if bits & place:
            out = out + place * (1 - 2 * ((index // place) % 2))
        place *= 2
    return out


def kernel(cfg, x_ref, counts_ref, partner_ref, out_ref, *scratch):
    nchan, groups, sizes, chosen, rounds, windows, width = cfg
    (tall, raw, cts, wgt, inv, sem_as, sem_ar, sem_ys, sem_yr, sem_bs, sem_br,
     sem_cs, sem_cr, sem_ts, sem_tr) = scratch[:15]
    nsub, bins = len(sizes), sum(sizes)
    starts = [sum(sizes[:s]) for s in range(nsub)]
    held, send = scratch[15:15 + nsub], scratch[15 + nsub:]
    total_bins = nchan * bins
    me = lax.axis_index("chan")
    mine = lax.axis_index("win")
    across, beside = flip(mine, 2), flip(mine, 1)
    rows = 2 * windows

    barrier = pltpu.get_barrier_semaphore()
    for d in range(1, nchan):
        pl.semaphore_signal(barrier, 1, device_id={"chan": flip(me, d)}, device_id_type=MESH)
    for d in range(1, groups):
        pl.semaphore_signal(barrier, 1, device_id={"win": flip(mine, d)}, device_id_type=MESH)

    def to_bins(s, d, peer=None):
        peer = flip(me, d) if peer is None else peer
        return pltpu.make_async_remote_copy(
            src_ref=send[s].at[peer], dst_ref=held[s].at[me, mine],
            send_sem=sem_as.at[s, d], recv_sem=sem_ar.at[s, d],
            device_id={"chan": peer}, device_id_type=MESH)

    half, quarter = nchan // 2, nchan // 4
    inner = ((me // half) + (me // quarter)) % 2

    def send_next(s, turn):
        d = nchan - turn
        peer = flip(me, d)
        if d >= half:
            peer = peer + inner * quarter * (1 - 2 * ((peer // quarter) % 2))
            d = d + inner * quarter * (1 - 2 * ((d // quarter) % 2))
        to_bins(s, d, peer).start()

    def to_across(s, d):
        block = held[s].at[flip(me, d), mine]
        return pltpu.make_async_remote_copy(
            src_ref=block, dst_ref=block, send_sem=sem_ys.at[s, d], recv_sem=sem_yr.at[s, d],
            device_id={"win": across}, device_id_type=MESH)

    def to_beside(s, d):
        block = held[s].at[flip(me, d), mine]
        return pltpu.make_async_remote_copy(
            src_ref=block, dst_ref=block, send_sem=sem_bs.at[s, d], recv_sem=sem_br.at[s, d],
            device_id={"win": beside}, device_id_type=MESH)

    def relay(s, d):
        block = held[s].at[flip(me, d), across]
        return pltpu.make_async_remote_copy(
            src_ref=block, dst_ref=block, send_sem=sem_cs.at[s, d], recv_sem=sem_cr.at[s, d],
            device_id={"win": beside}, device_id_type=MESH)

    def tallies(d):
        return pltpu.make_async_remote_copy(
            src_ref=tall.at[mine], dst_ref=tall.at[mine],
            send_sem=sem_ts.at[d], recv_sem=sem_tr.at[d],
            device_id={"win": flip(mine, d)}, device_id_type=MESH)

    def add_power(f, acc):
        v = x_ref[f].astype(jnp.float32)
        return acc + v * v

    acc = lax.fori_loop(0, total_bins, add_power, jnp.zeros((rows, width), jnp.float32), unroll=4)
    raw[0] = acc
    power = (raw[0, pl.ds(0, windows, stride=2), :] + raw[0, pl.ds(1, windows, stride=2), :]) * (1.0 / total_bins)
    scale = lax.rsqrt(power + EPS)

    def whiten(s):
        def one(j, carry):
            for q in range(sizes[s]):
                raw[q] = x_ref[j * bins + starts[s] + q].astype(jnp.float32)
            for q in range(sizes[s]):
                for k in range(2):
                    part = raw[q, pl.ds(k, windows, stride=2), :] * scale
                    send[s][j, q, pl.ds(k * windows, windows), :] = part.astype(jnp.bfloat16)
            return carry

        lax.fori_loop(0, nchan, one, 0)
        held[s][me, mine] = send[s][me]

    tall[mine] = jnp.zeros(tall.shape[1:], jnp.float32)
    tall[mine, :, pl.ds(0, windows)] = counts_ref[...].astype(jnp.float32)

    whiten(0)
    pl.semaphore_wait(barrier, nchan - 1 + groups - 1)
    to_across(0, 0).start()
    to_beside(0, 0).start()
    for turn in range(1, nchan):
        send_next(0, turn)
    for d in range(1, groups):
        tallies(d).start()
    for s in range(1, AHEAD):
        whiten(s)
        for turn in range(1, nchan):
            send_next(s, turn)

    def weights():
        for d in range(1, groups):
            tallies(d).wait_recv()
        whole = tall[0]
        for g in range(1, groups):
            whole = whole + pltpu.roll(tall[g], g * windows, 1)
        cts[...] = whole
        first = mine * chosen

        def one(n, carry):
            own = cts[pl.ds(first + n, 1), :]
            for r in range(rounds):
                row = jnp.minimum(own, cts[pl.ds(partner_ref[r, first + n], 1), :]) * (1.0 / NSAMP)
                wgt[n, r] = jnp.broadcast_to(row, (LANES, LANES)).T.astype(jnp.bfloat16)
                norm = lax.rsqrt(jnp.sum(row * row, axis=1, keepdims=True))
                inv[n, r] = jnp.broadcast_to(norm, (8, width))
            return carry

        lax.fori_loop(0, chosen, one, 0)

    def planes(s, block, q):
        return [
            jnp.concatenate(
                [held[s][block, g, q, pl.ds(k * windows, windows), :] for g in range(groups)], axis=0)
            for k in range(2)
        ]

    def unit(s, u):
        n, q = u // sizes[s], u % sizes[s]
        a = mine * chosen + n
        re, im = planes(s, a, q)
        re, im = re.T, im.T
        lhs = jnp.concatenate(
            [jnp.concatenate([re, im], axis=1), jnp.concatenate([im, -re], axis=1)], axis=0)
        mates = []
        for r in range(rounds):
            w = wgt[n, r]
            mre, mim = planes(s, partner_ref[r, a], q)
            mates.append(jnp.concatenate([mre * w, mim * w], axis=0))
        rhs = jnp.concatenate(mates, axis=1)
        res = jnp.dot(lhs, rhs, preferred_element_type=jnp.float32)
        for r in range(rounds):
            norm = inv[n, r, pl.ds(0, 1), :]
            for k in range(2):
                tile = res[k * width:(k + 1) * width, r * width:(r + 1) * width] * norm
                out_ref[n, r, starts[s] + q, :, pl.ds(k * width, width)] = tile.astype(jnp.bfloat16)

    def compute(s, low, high):
        lax.fori_loop(low, high, lambda u, carry: (unit(s, u), carry)[1], 0, unroll=2 if (high - low) % 2 == 0 else 1)

    def settle(s):
        for d in range(nchan):
            to_beside(s, d).wait_recv()
            relay(s, d).wait_recv()

    def pass_on(step):
        s, d = step // nchan, step % nchan
        to_across(s, d).wait_recv()
        relay(s, d).start()

    lag = nchan // 2
    late = 5 * nchan // 8
    for s in range(nsub):
        units = chosen * sizes[s - 1]
        for d in range(nchan):
            step = s * nchan + d
            if d:
                to_bins(s, d).wait_recv()
            if step:
                to_across(s, d).start()
                to_beside(s, d).start()
            if d == 0 and s + AHEAD < nsub:
                whiten(s + AHEAD)
            if d and s + AHEAD < nsub:
                send_next(s + AHEAD, d)
            if step >= lag:
                pass_on(step - lag)
            if step == nchan - 1:
                weights()
            if s and d >= late:
                if d == late:
                    settle(s - 1)
                i = d - late
                compute(s - 1, i * units // (nchan - late), (i + 1) * units // (nchan - late))
    for step in range(nsub * nchan - lag, nsub * nchan):
        pass_on(step)
    settle(nsub - 1)
    compute(nsub - 1, 0, chosen * sizes[-1])

    for d in range(1, groups):
        tallies(d).wait_send()
    for s in range(nsub):
        for d in range(nchan):
            if d:
                to_bins(s, d).wait_send()
            to_across(s, d).wait_send()
            to_beside(s, d).wait_send()
            relay(s, d).wait_send()


def per_device(nchan, groups, spectra, counts, partner):
    _, total_bins, windows, parts, width = spectra.shape
    rounds, nblocks = partner.shape
    bins = total_bins // nchan
    chosen = nblocks // groups
    sizes = (bins // 4,) * 3 + (bins // 8,) * 2 if bins % 8 == 0 else (1,) * bins
    nsub = len(sizes)
    cfg = (nchan, groups, sizes, chosen, rounds, windows, width)
    x = spectra.reshape(total_bins, windows * parts, width)
    dma = pltpu.SemaphoreType.DMA
    flops = 2 * chosen * rounds * bins * width * (2 * width) * (2 * groups * windows)
    return pl.pallas_call(
        functools.partial(kernel, cfg),
        out_shape=jax.ShapeDtypeStruct((chosen, rounds, bins, width, 2 * width), jnp.bfloat16),
        in_specs=[
            pl.BlockSpec(memory_space=pltpu.VMEM),
            pl.BlockSpec(memory_space=pltpu.VMEM),
            pl.BlockSpec(memory_space=pltpu.SMEM),
        ],
        out_specs=pl.BlockSpec(memory_space=pltpu.VMEM),
        scratch_shapes=[
            pltpu.VMEM((groups, nblocks, LANES), jnp.float32),
            pltpu.VMEM((max(sizes), 2 * windows, width), jnp.float32),
            pltpu.VMEM((nblocks, LANES), jnp.float32),
            pltpu.VMEM((chosen, rounds, groups * windows, width), jnp.bfloat16),
            pltpu.VMEM((chosen, rounds, 8, width), jnp.float32),
        ]
        + [dma((nsub, nchan))] * 8
        + [dma((groups,))] * 2
        + [pltpu.VMEM((nblocks, groups, size, 2 * windows, width), jnp.bfloat16) for size in sizes]
        + [pltpu.VMEM((nchan, size, 2 * windows, width), jnp.bfloat16) for size in sizes],
        compiler_params=pltpu.CompilerParams(
            collective_id=0, has_side_effects=True, vmem_limit_bytes=40 * 1024 * 1024),
        cost_estimate=pl.CostEstimate(flops=flops, bytes_accessed=8 << 20, transcendentals=0),
    )(x, counts.T, partner)


def solution(mesh):
    sizes = dict(mesh.shape)
    placed = (P("chan", None, "win", None, None), P("win", None), P())
    return jax.shard_map(
        functools.partial(per_device, sizes["chan"], sizes["win"]),
        mesh=mesh,
        in_specs=placed,
        out_specs=P("win", None, "chan", None, None),
        check_vma=False,
    )
```

```python
import functools

import jax
import jax.numpy as jnp
from jax import lax
from jax.experimental import pallas as pl
from jax.experimental.pallas import tpu as pltpu
from jax.sharding import PartitionSpec as P

NSAMP = 256
EPS = 1e-06
LANES = 128
AHEAD = 2
MESH = pl.DeviceIdType.MESH


def flip(index, bits):
    out, place = index, 1
    while place <= bits:
        if bits & place:
            out = out + place * (1 - 2 * ((index // place) % 2))
        place *= 2
    return out


def kernel(cfg, x_ref, counts_ref, partner_ref, out_ref, *scratch):
    nchan, groups, sizes, chosen, rounds, windows, width = cfg
    (tall, raw, cts, wgt, inv, sem_as, sem_ar, sem_ys, sem_yr, sem_bs, sem_br,
     sem_cs, sem_cr, sem_ts, sem_tr) = scratch[:15]
    nsub, bins = len(sizes), sum(sizes)
    starts = [sum(sizes[:s]) for s in range(nsub)]
    held, send = scratch[15:15 + nsub], scratch[15 + nsub:]
    total_bins = nchan * bins
    me = lax.axis_index("chan")
    mine = lax.axis_index("win")
    across, beside = flip(mine, 2), flip(mine, 1)
    rows = 2 * windows

    barrier = pltpu.get_barrier_semaphore()
    for d in range(1, nchan):
        pl.semaphore_signal(barrier, 1, device_id={"chan": flip(me, d)}, device_id_type=MESH)
    for d in range(1, groups):
        pl.semaphore_signal(barrier, 1, device_id={"win": flip(mine, d)}, device_id_type=MESH)

    def to_bins(s, d, peer=None):
        peer = flip(me, d) if peer is None else peer
        return pltpu.make_async_remote_copy(
            src_ref=send[s].at[peer], dst_ref=held[s].at[me, mine],
            send_sem=sem_as.at[s, d], recv_sem=sem_ar.at[s, d],
            device_id={"chan": peer}, device_id_type=MESH)

    half, quarter = nchan // 2, nchan // 4
    inner = ((me // half) + (me // quarter)) % 2

    def send_one(s, d):
        peer = flip(me, d)
        if d >= half:
            peer = peer + inner * quarter * (1 - 2 * ((peer // quarter) % 2))
            d = d + inner * quarter * (1 - 2 * ((d // quarter) % 2))
        to_bins(s, d, peer).start()

    near, far = range(1, half), range(nchan - 1, half - 1, -1)

    def send_all(s):
        for d in (*near, *far):
            send_one(s, d)

    def to_across(s, d):
        block = held[s].at[flip(me, d), mine]
        return pltpu.make_async_remote_copy(
            src_ref=block, dst_ref=block, send_sem=sem_ys.at[s, d], recv_sem=sem_yr.at[s, d],
            device_id={"win": across}, device_id_type=MESH)

    def to_beside(s, d):
        block = held[s].at[flip(me, d), mine]
        return pltpu.make_async_remote_copy(
            src_ref=block, dst_ref=block, send_sem=sem_bs.at[s, d], recv_sem=sem_br.at[s, d],
            device_id={"win": beside}, device_id_type=MESH)

    def relay(s, d):
        block = held[s].at[flip(me, d), across]
        return pltpu.make_async_remote_copy(
            src_ref=block, dst_ref=block, send_sem=sem_cs.at[s, d], recv_sem=sem_cr.at[s, d],
            device_id={"win": beside}, device_id_type=MESH)

    def tallies(d):
        return pltpu.make_async_remote_copy(
            src_ref=tall.at[mine], dst_ref=tall.at[mine],
            send_sem=sem_ts.at[d], recv_sem=sem_tr.at[d],
            device_id={"win": flip(mine, d)}, device_id_type=MESH)

    def add_power(f, acc):
        v = x_ref[f].astype(jnp.float32)
        return acc + v * v

    acc = lax.fori_loop(0, total_bins, add_power, jnp.zeros((rows, width), jnp.float32), unroll=4)
    raw[0] = acc
    power = (raw[0, pl.ds(0, windows, stride=2), :] + raw[0, pl.ds(1, windows, stride=2), :]) * (1.0 / total_bins)
    scale = lax.rsqrt(power + EPS)

    def whiten(s):
        def one(j, carry):
            for q in range(sizes[s]):
                raw[q] = x_ref[j * bins + starts[s] + q].astype(jnp.float32)
            for q in range(sizes[s]):
                for k in range(2):
                    part = raw[q, pl.ds(k, windows, stride=2), :] * scale
                    send[s][j, q, pl.ds(k * windows, windows), :] = part.astype(jnp.bfloat16)
            return carry

        lax.fori_loop(0, nchan, one, 0)
        held[s][me, mine] = send[s][me]

    tall[mine] = jnp.zeros(tall.shape[1:], jnp.float32)
    tall[mine, :, pl.ds(0, windows)] = counts_ref[...].astype(jnp.float32)

    whiten(0)
    pl.semaphore_wait(barrier, nchan - 1 + groups - 1)
    to_across(0, 0).start()
    to_beside(0, 0).start()
    send_all(0)
    for d in range(1, groups):
        tallies(d).start()
    for s in range(1, min(AHEAD, nsub)):
        whiten(s)
        send_all(s)

    def weights():
        for d in range(1, groups):
            tallies(d).wait_recv()
        whole = tall[0]
        for g in range(1, groups):
            whole = whole + pltpu.roll(tall[g], g * windows, 1)
        cts[...] = whole
        first = mine * chosen

        def one(n, carry):
            own = cts[pl.ds(first + n, 1), :]
            for r in range(rounds):
                row = jnp.minimum(own, cts[pl.ds(partner_ref[r, first + n], 1), :]) * (1.0 / NSAMP)
                wgt[n, r] = jnp.broadcast_to(row, (LANES, LANES)).T.astype(jnp.bfloat16)
                norm = lax.rsqrt(jnp.sum(row * row, axis=1, keepdims=True))
                inv[n, r] = jnp.broadcast_to(norm, (8, width))
            return carry

        lax.fori_loop(0, chosen, one, 0)

    def planes(s, block, q):
        return [
            jnp.concatenate(
                [held[s][block, g, q, pl.ds(k * windows, windows), :] for g in range(groups)], axis=0)
            for k in range(2)
        ]

    def unit(s, u):
        n, q = u // sizes[s], u % sizes[s]
        a = mine * chosen + n
        re, im = planes(s, a, q)
        re, im = re.T, im.T
        lhs = jnp.concatenate(
            [jnp.concatenate([re, im], axis=1), jnp.concatenate([im, -re], axis=1)], axis=0)
        mates = []
        for r in range(rounds):
            w = wgt[n, r]
            mre, mim = planes(s, partner_ref[r, a], q)
            mates.append(jnp.concatenate([mre * w, mim * w], axis=0))
        rhs = jnp.concatenate(mates, axis=1)
        res = jnp.dot(lhs, rhs, preferred_element_type=jnp.float32)
        for r in range(rounds):
            norm = inv[n, r, pl.ds(0, 1), :]
            for k in range(2):
                tile = res[k * width:(k + 1) * width, r * width:(r + 1) * width] * norm
                out_ref[n, r, starts[s] + q, :, pl.ds(k * width, width)] = tile.astype(jnp.bfloat16)

    def compute(s, low, high):
        lax.fori_loop(low, high, lambda u, carry: (unit(s, u), carry)[1], 0, unroll=2 if (high - low) % 2 == 0 else 1)

    def settle(s):
        for d in range(nchan):
            to_beside(s, d).wait_recv()
            relay(s, d).wait_recv()

    order = [(0, d) for d in range(half)]
    for s in range(nsub):
        if s + 1 < nsub:
            order += [(s + 1, d) for d in range(half)]
        order += [(s, d) for d in range(half, nchan)]

    def pass_on(s, d):
        to_across(s, d).wait_recv()
        relay(s, d).start()

    def share(s, i, count):
        units = chosen * sizes[s]
        compute(s, i * units // count, (i + 1) * units // count)

    lag = half
    skip = half // 4
    for step, (s, d) in enumerate(order):
        if d:
            to_bins(s, d).wait_recv()
        if step:
            to_across(s, d).start()
            to_beside(s, d).start()
        if d == 0 and 0 < s < nsub - 1:
            whiten(s + 1)
            for e in near:
                send_one(s + 1, e)
        if d >= half and s + AHEAD < nsub:
            send_one(s + AHEAD, nchan - 1 - (d - half))
        if step >= lag:
            pass_on(*order[step - lag])
        if step == nchan - 1:
            weights()
        if 0 < s < nsub - 1 and d >= half + skip:
            if d == half + skip:
                settle(s - 1)
            share(s - 1, d - half - skip, half - skip)
    for i, (s, d) in enumerate(order[-lag:]):
        pass_on(s, d)
        if nsub > 1:
            if i == 0:
                settle(nsub - 2)
            share(nsub - 2, i, lag)
    settle(nsub - 1)
    share(nsub - 1, 0, 1)

    for d in range(1, groups):
        tallies(d).wait_send()
    for s in range(nsub):
        for d in range(nchan):
            if d:
                to_bins(s, d).wait_send()
            to_across(s, d).wait_send()
            to_beside(s, d).wait_send()
            relay(s, d).wait_send()


def per_device(nchan, groups, spectra, counts, partner):
    _, total_bins, windows, parts, width = spectra.shape
    rounds, nblocks = partner.shape
    bins = total_bins // nchan
    chosen = nblocks // groups
    sizes = (bins // 4,) * 3 + (bins // 8,) * 2 if bins % 8 == 0 else (1,) * bins
    nsub = len(sizes)
    cfg = (nchan, groups, sizes, chosen, rounds, windows, width)
    x = spectra.reshape(total_bins, windows * parts, width)
    dma = pltpu.SemaphoreType.DMA
    flops = 2 * chosen * rounds * bins * width * (2 * width) * (2 * groups * windows)
    return pl.pallas_call(
        functools.partial(kernel, cfg),
        out_shape=jax.ShapeDtypeStruct((chosen, rounds, bins, width, 2 * width), jnp.bfloat16),
        in_specs=[
            pl.BlockSpec(memory_space=pltpu.VMEM),
            pl.BlockSpec(memory_space=pltpu.VMEM),
            pl.BlockSpec(memory_space=pltpu.SMEM),
        ],
        out_specs=pl.BlockSpec(memory_space=pltpu.VMEM),
        scratch_shapes=[
            pltpu.VMEM((groups, nblocks, LANES), jnp.float32),
            pltpu.VMEM((max(sizes), 2 * windows, width), jnp.float32),
            pltpu.VMEM((nblocks, LANES), jnp.float32),
            pltpu.VMEM((chosen, rounds, groups * windows, width), jnp.bfloat16),
            pltpu.VMEM((chosen, rounds, 8, width), jnp.float32),
        ]
        + [dma((nsub, nchan))] * 8
        + [dma((groups,))] * 2
        + [pltpu.VMEM((nblocks, groups, size, 2 * windows, width), jnp.bfloat16) for size in sizes]
        + [pltpu.VMEM((nchan, size, 2 * windows, width), jnp.bfloat16) for size in sizes],
        compiler_params=pltpu.CompilerParams(
            collective_id=0, has_side_effects=True, vmem_limit_bytes=40 * 1024 * 1024),
        cost_estimate=pl.CostEstimate(flops=flops, bytes_accessed=8 << 20, transcendentals=0),
    )(x, counts.T, partner)


def solution(mesh):
    sizes = dict(mesh.shape)
    placed = (P("chan", None, "win", None, None), P("win", None), P())
    return jax.shard_map(
        functools.partial(per_device, sizes["chan"], sizes["win"]),
        mesh=mesh,
        in_specs=placed,
        out_specs=P("win", None, "chan", None, None),
        check_vma=False,
    )
```

```python
import functools

import jax
import jax.numpy as jnp
from jax import lax
from jax.experimental import pallas as pl
from jax.experimental.pallas import tpu as pltpu
from jax.sharding import PartitionSpec as P

NSAMP = 256
EPS = 1e-06
LANES = 128
MESH = pl.DeviceIdType.MESH


def flip(index, bits):
    out, place = index, 1
    while place <= bits:
        if bits & place:
            out = out + place * (1 - 2 * ((index // place) % 2))
        place *= 2
    return out


def kernel(cfg, x_ref, counts_ref, partner_ref, out_ref, *scratch):
    nchan, groups, sizes, chosen, rounds, windows, width = cfg
    (tall, raw, cts, wgt, inv, sem_as, sem_ar, sem_ys, sem_yr, sem_bs, sem_br,
     sem_cs, sem_cr, sem_ts, sem_tr) = scratch[:15]
    nsub, bins = len(sizes), sum(sizes)
    starts = [sum(sizes[:s]) for s in range(nsub)]
    held, send = scratch[15:15 + nsub], scratch[15 + nsub:]
    total_bins = nchan * bins
    me = lax.axis_index("chan")
    mine = lax.axis_index("win")
    across, beside = flip(mine, 2), flip(mine, 1)
    rows = 2 * windows

    barrier = pltpu.get_barrier_semaphore()
    for d in range(1, nchan):
        pl.semaphore_signal(barrier, 1, device_id={"chan": flip(me, d)}, device_id_type=MESH)
    for d in range(1, groups):
        pl.semaphore_signal(barrier, 1, device_id={"win": flip(mine, d)}, device_id_type=MESH)

    def to_bins(s, d, peer=None):
        peer = flip(me, d) if peer is None else peer
        return pltpu.make_async_remote_copy(
            src_ref=send[s].at[peer], dst_ref=held[s].at[me, mine],
            send_sem=sem_as.at[s, d], recv_sem=sem_ar.at[s, d],
            device_id={"chan": peer}, device_id_type=MESH)

    half, quarter = nchan // 2, nchan // 4
    inner = ((me // half) + (me // quarter)) % 2

    def send_one(s, d):
        peer = flip(me, d)
        if d >= half:
            peer = peer + inner * quarter * (1 - 2 * ((peer // quarter) % 2))
            d = d + inner * quarter * (1 - 2 * ((d // quarter) % 2))
        to_bins(s, d, peer).start()

    near, far = range(1, half), range(nchan - 1, half - 1, -1)

    def send_part(s, part):
        for d in part:
            send_one(s, d)

    def to_across(s, d):
        block = held[s].at[flip(me, d), mine]
        return pltpu.make_async_remote_copy(
            src_ref=block, dst_ref=block, send_sem=sem_ys.at[s, d], recv_sem=sem_yr.at[s, d],
            device_id={"win": across}, device_id_type=MESH)

    def to_beside(s, d):
        block = held[s].at[flip(me, d), mine]
        return pltpu.make_async_remote_copy(
            src_ref=block, dst_ref=block, send_sem=sem_bs.at[s, d], recv_sem=sem_br.at[s, d],
            device_id={"win": beside}, device_id_type=MESH)

    def relay(s, d):
        block = held[s].at[flip(me, d), across]
        return pltpu.make_async_remote_copy(
            src_ref=block, dst_ref=block, send_sem=sem_cs.at[s, d], recv_sem=sem_cr.at[s, d],
            device_id={"win": beside}, device_id_type=MESH)

    def tallies(d):
        return pltpu.make_async_remote_copy(
            src_ref=tall.at[mine], dst_ref=tall.at[mine],
            send_sem=sem_ts.at[d], recv_sem=sem_tr.at[d],
            device_id={"win": flip(mine, d)}, device_id_type=MESH)

    def add_power(f, acc):
        v = x_ref[f].astype(jnp.float32)
        return acc + v * v

    acc = lax.fori_loop(0, total_bins, add_power, jnp.zeros((rows, width), jnp.float32), unroll=4)
    raw[0] = acc
    power = (raw[0, pl.ds(0, windows, stride=2), :] + raw[0, pl.ds(1, windows, stride=2), :]) * (1.0 / total_bins)
    scale = lax.rsqrt(power + EPS)

    def whiten(s):
        def one(j, carry):
            for q in range(sizes[s]):
                raw[q] = x_ref[j * bins + starts[s] + q].astype(jnp.float32)
            for q in range(sizes[s]):
                for k in range(2):
                    part = raw[q, pl.ds(k, windows, stride=2), :] * scale
                    send[s][j, q, pl.ds(k * windows, windows), :] = part.astype(jnp.bfloat16)
            return carry

        lax.fori_loop(0, nchan, one, 0)
        held[s][me, mine] = send[s][me]

    tall[mine] = jnp.zeros(tall.shape[1:], jnp.float32)
    tall[mine, :, pl.ds(0, windows)] = counts_ref[...].astype(jnp.float32)

    whiten(0)
    pl.semaphore_wait(barrier, nchan - 1 + groups - 1)
    to_across(0, 0).start()
    to_beside(0, 0).start()
    send_part(0, near)
    for d in range(1, groups):
        tallies(d).start()
    if nsub > 1:
        whiten(1)
        send_part(1, near)
    send_part(0, far)

    def weights():
        for d in range(1, groups):
            tallies(d).wait_recv()
        whole = tall[0]
        for g in range(1, groups):
            whole = whole + pltpu.roll(tall[g], g * windows, 1)
        cts[...] = whole
        first = mine * chosen

        def one(n, carry):
            own = cts[pl.ds(first + n, 1), :]
            for r in range(rounds):
                row = jnp.minimum(own, cts[pl.ds(partner_ref[r, first + n], 1), :]) * (1.0 / NSAMP)
                wgt[n, r] = jnp.broadcast_to(row, (LANES, LANES)).T.astype(jnp.bfloat16)
                norm = lax.rsqrt(jnp.sum(row * row, axis=1, keepdims=True))
                inv[n, r] = jnp.broadcast_to(norm, (8, width))
            return carry

        lax.fori_loop(0, chosen, one, 0)

    def planes(s, block, q):
        return [
            jnp.concatenate(
                [held[s][block, g, q, pl.ds(k * windows, windows), :] for g in range(groups)], axis=0)
            for k in range(2)
        ]

    def unit(s, u):
        n, q = u // sizes[s], u % sizes[s]
        a = mine * chosen + n
        re, im = planes(s, a, q)
        re, im = re.T, im.T
        lhs = jnp.concatenate(
            [jnp.concatenate([re, im], axis=1), jnp.concatenate([im, -re], axis=1)], axis=0)
        mates = []
        for r in range(rounds):
            w = wgt[n, r]
            mre, mim = planes(s, partner_ref[r, a], q)
            mates.append(jnp.concatenate([mre * w, mim * w], axis=0))
        rhs = jnp.concatenate(mates, axis=1)
        res = jnp.dot(lhs, rhs, preferred_element_type=jnp.float32)
        for r in range(rounds):
            norm = inv[n, r, pl.ds(0, 1), :]
            for k in range(2):
                tile = res[k * width:(k + 1) * width, r * width:(r + 1) * width] * norm
                out_ref[n, r, starts[s] + q, :, pl.ds(k * width, width)] = tile.astype(jnp.bfloat16)

    def compute(s, low, high):
        lax.fori_loop(low, high, lambda u, carry: (unit(s, u), carry)[1], 0, unroll=2 if (high - low) % 2 == 0 else 1)

    def settle(s):
        for d in range(nchan):
            to_beside(s, d).wait_recv()
            relay(s, d).wait_recv()

    order = [(0, d) for d in range(half)]
    for s in range(nsub):
        if s + 1 < nsub:
            order += [(s + 1, d) for d in range(half)]
        order += [(s, d) for d in range(half, nchan)]

    def pass_on(s, d):
        to_across(s, d).wait_recv()
        relay(s, d).start()

    def share(s, i, count):
        units = chosen * sizes[s]
        compute(s, i * units // count, (i + 1) * units // count)

    lag = half
    skip = half // 4
    for step, (s, d) in enumerate(order):
        if d:
            to_bins(s, d).wait_recv()
        if step:
            to_across(s, d).start()
            to_beside(s, d).start()
        if step == 1:
            if nsub > 2:
                whiten(2)
                send_part(2, near)
            if nsub > 1:
                send_part(1, far)
        if d == half and s + 3 < nsub:
            whiten(s + 3)
            send_part(s + 3, near)
        if d >= half and s + 2 < nsub:
            send_one(s + 2, nchan - 1 - (d - half))
        if step >= lag:
            pass_on(*order[step - lag])
        if step == nchan - 1:
            weights()
        if 0 < s < nsub - 1 and d >= half + skip:
            if d == half + skip:
                settle(s - 1)
            share(s - 1, d - half - skip, half - skip)
    for i, (s, d) in enumerate(order[-lag:]):
        pass_on(s, d)
        if nsub > 1:
            if i == 0:
                settle(nsub - 2)
            share(nsub - 2, i, lag)
    settle(nsub - 1)
    share(nsub - 1, 0, 1)

    for d in range(1, groups):
        tallies(d).wait_send()
    for s in range(nsub):
        for d in range(nchan):
            if d:
                to_bins(s, d).wait_send()
            to_across(s, d).wait_send()
            to_beside(s, d).wait_send()
            relay(s, d).wait_send()


def per_device(nchan, groups, spectra, counts, partner):
    _, total_bins, windows, parts, width = spectra.shape
    rounds, nblocks = partner.shape
    bins = total_bins // nchan
    chosen = nblocks // groups
    sizes = (bins // 4,) * 3 + (bins // 8,) * 2 if bins % 8 == 0 else (1,) * bins
    nsub = len(sizes)
    cfg = (nchan, groups, sizes, chosen, rounds, windows, width)
    x = spectra.reshape(total_bins, windows * parts, width)
    dma = pltpu.SemaphoreType.DMA
    flops = 2 * chosen * rounds * bins * width * (2 * width) * (2 * groups * windows)
    return pl.pallas_call(
        functools.partial(kernel, cfg),
        out_shape=jax.ShapeDtypeStruct((chosen, rounds, bins, width, 2 * width), jnp.bfloat16),
        in_specs=[
            pl.BlockSpec(memory_space=pltpu.VMEM),
            pl.BlockSpec(memory_space=pltpu.VMEM),
            pl.BlockSpec(memory_space=pltpu.SMEM),
        ],
        out_specs=pl.BlockSpec(memory_space=pltpu.VMEM),
        scratch_shapes=[
            pltpu.VMEM((groups, nblocks, LANES), jnp.float32),
            pltpu.VMEM((max(sizes), 2 * windows, width), jnp.float32),
            pltpu.VMEM((nblocks, LANES), jnp.float32),
            pltpu.VMEM((chosen, rounds, groups * windows, width), jnp.bfloat16),
            pltpu.VMEM((chosen, rounds, 8, width), jnp.float32),
        ]
        + [dma((nsub, nchan))] * 8
        + [dma((groups,))] * 2
        + [pltpu.VMEM((nblocks, groups, size, 2 * windows, width), jnp.bfloat16) for size in sizes]
        + [pltpu.VMEM((nchan, size, 2 * windows, width), jnp.bfloat16) for size in sizes],
        compiler_params=pltpu.CompilerParams(
            collective_id=0, has_side_effects=True, vmem_limit_bytes=40 * 1024 * 1024),
        cost_estimate=pl.CostEstimate(flops=flops, bytes_accessed=8 << 20, transcendentals=0),
    )(x, counts.T, partner)


def solution(mesh):
    sizes = dict(mesh.shape)
    placed = (P("chan", None, "win", None, None), P("win", None), P())
    return jax.shard_map(
        functools.partial(per_device, sizes["chan"], sizes["win"]),
        mesh=mesh,
        in_specs=placed,
        out_specs=P("win", None, "chan", None, None),
        check_vma=False,
    )
```

```python
import functools

import jax
import jax.numpy as jnp
from jax import lax
from jax.experimental import pallas as pl
from jax.experimental.pallas import tpu as pltpu
from jax.sharding import PartitionSpec as P

NSAMP = 256
EPS = 1e-06
LANES = 128
MESH = pl.DeviceIdType.MESH


def flip(index, bits):
    out, place = index, 1
    while place <= bits:
        if bits & place:
            out = out + place * (1 - 2 * ((index // place) % 2))
        place *= 2
    return out


def kernel(cfg, x_ref, counts_ref, partner_ref, out_ref, *scratch):
    nchan, groups, sizes, chosen, rounds, windows, width = cfg
    (tall, raw, cts, wgt, inv, sem_as, sem_ar, sem_ys, sem_yr, sem_bs, sem_br,
     sem_cs, sem_cr, sem_ts, sem_tr) = scratch[:15]
    nsub, bins = len(sizes), sum(sizes)
    starts = [sum(sizes[:s]) for s in range(nsub)]
    held, send = scratch[15:15 + nsub], scratch[15 + nsub:]
    total_bins = nchan * bins
    me = lax.axis_index("chan")
    mine = lax.axis_index("win")
    across, beside = flip(mine, 2), flip(mine, 1)
    rows = 2 * windows

    barrier = pltpu.get_barrier_semaphore()
    for d in range(1, nchan):
        pl.semaphore_signal(barrier, 1, device_id={"chan": flip(me, d)}, device_id_type=MESH)
    for d in range(1, groups):
        pl.semaphore_signal(barrier, 1, device_id={"win": flip(mine, d)}, device_id_type=MESH)

    def to_bins(s, d, peer=None):
        peer = flip(me, d) if peer is None else peer
        return pltpu.make_async_remote_copy(
            src_ref=send[s].at[peer], dst_ref=held[s].at[me, mine],
            send_sem=sem_as.at[s, d], recv_sem=sem_ar.at[s, d],
            device_id={"chan": peer}, device_id_type=MESH)

    half, quarter = nchan // 2, nchan // 4
    inner = ((me // half) + (me // quarter)) % 2

    def send_one(s, d):
        peer = flip(me, d)
        if d >= half:
            peer = peer + inner * quarter * (1 - 2 * ((peer // quarter) % 2))
            d = d + inner * quarter * (1 - 2 * ((d // quarter) % 2))
        to_bins(s, d, peer).start()

    near, far = range(1, half), range(nchan - 1, half - 1, -1)

    def send_part(s, part):
        for d in part:
            send_one(s, d)

    def to_across(s, d):
        block = held[s].at[flip(me, d), mine]
        return pltpu.make_async_remote_copy(
            src_ref=block, dst_ref=block, send_sem=sem_ys.at[s, d], recv_sem=sem_yr.at[s, d],
            device_id={"win": across}, device_id_type=MESH)

    def to_beside(s, d):
        block = held[s].at[flip(me, d), mine]
        return pltpu.make_async_remote_copy(
            src_ref=block, dst_ref=block, send_sem=sem_bs.at[s, d], recv_sem=sem_br.at[s, d],
            device_id={"win": beside}, device_id_type=MESH)

    def relay(s, d):
        block = held[s].at[flip(me, d), across]
        return pltpu.make_async_remote_copy(
            src_ref=block, dst_ref=block, send_sem=sem_cs.at[s, d], recv_sem=sem_cr.at[s, d],
            device_id={"win": beside}, device_id_type=MESH)

    def tallies(d):
        return pltpu.make_async_remote_copy(
            src_ref=tall.at[mine], dst_ref=tall.at[mine],
            send_sem=sem_ts.at[d], recv_sem=sem_tr.at[d],
            device_id={"win": flip(mine, d)}, device_id_type=MESH)

    def add_power(f, acc):
        v = x_ref[f].astype(jnp.float32)
        return acc + v * v

    acc = lax.fori_loop(0, total_bins, add_power, jnp.zeros((rows, width), jnp.float32), unroll=4)
    raw[0] = acc
    power = (raw[0, pl.ds(0, windows, stride=2), :] + raw[0, pl.ds(1, windows, stride=2), :]) * (1.0 / total_bins)
    scale = lax.rsqrt(power + EPS)

    def whiten(s):
        def one(j, carry):
            for q in range(sizes[s]):
                raw[q] = x_ref[j * bins + starts[s] + q].astype(jnp.float32)
            for q in range(sizes[s]):
                for k in range(2):
                    part = raw[q, pl.ds(k, windows, stride=2), :] * scale
                    send[s][j, q, pl.ds(k * windows, windows), :] = part.astype(jnp.bfloat16)
            return carry

        lax.fori_loop(0, nchan, one, 0)
        held[s][me, mine] = send[s][me]

    tall[mine] = jnp.zeros(tall.shape[1:], jnp.float32)
    tall[mine, :, pl.ds(0, windows)] = counts_ref[...].astype(jnp.float32)

    whiten(0)
    pl.semaphore_wait(barrier, nchan - 1 + groups - 1)
    to_across(0, 0).start()
    to_beside(0, 0).start()
    send_part(0, near)
    for d in range(1, groups):
        tallies(d).start()
    if nsub > 1:
        whiten(1)
        send_part(1, near)
    send_part(0, far)

    def weights():
        for d in range(1, groups):
            tallies(d).wait_recv()
        whole = tall[0]
        for g in range(1, groups):
            whole = whole + pltpu.roll(tall[g], g * windows, 1)
        cts[...] = whole
        first = mine * chosen

        def one(n, carry):
            own = cts[pl.ds(first + n, 1), :]
            for r in range(rounds):
                row = jnp.minimum(own, cts[pl.ds(partner_ref[r, first + n], 1), :]) * (1.0 / NSAMP)
                wgt[n, r] = jnp.broadcast_to(row, (LANES, LANES)).T.astype(jnp.bfloat16)
                norm = lax.rsqrt(jnp.sum(row * row, axis=1, keepdims=True))
                inv[n, r] = jnp.broadcast_to(norm, (8, width))
            return carry

        lax.fori_loop(0, chosen, one, 0)

    def planes(s, block, q):
        return [
            jnp.concatenate(
                [held[s][block, g, q, pl.ds(k * windows, windows), :] for g in range(groups)], axis=0)
            for k in range(2)
        ]

    def unit(s, u):
        n, q = u // sizes[s], u % sizes[s]
        a = mine * chosen + n
        re, im = planes(s, a, q)
        re, im = re.T, im.T
        lhs = jnp.concatenate(
            [jnp.concatenate([re, im], axis=1), jnp.concatenate([im, -re], axis=1)], axis=0)
        mates = []
        for r in range(rounds):
            w = wgt[n, r]
            mre, mim = planes(s, partner_ref[r, a], q)
            mates.append(jnp.concatenate([mre * w, mim * w], axis=0))
        rhs = jnp.concatenate(mates, axis=1)
        res = jnp.dot(lhs, rhs, preferred_element_type=jnp.float32)
        for r in range(rounds):
            norm = inv[n, r, pl.ds(0, 1), :]
            for k in range(2):
                tile = res[k * width:(k + 1) * width, r * width:(r + 1) * width] * norm
                out_ref[n, r, starts[s] + q, :, pl.ds(k * width, width)] = tile.astype(jnp.bfloat16)

    def compute(s, low, high):
        lax.fori_loop(low, high, lambda u, carry: (unit(s, u), carry)[1], 0, unroll=2 if (high - low) % 2 == 0 else 1)

    def settle(s):
        for d in range(nchan):
            to_beside(s, d).wait_recv()
            relay(s, d).wait_recv()

    order = [(0, d) for d in range(half)]
    for s in range(nsub):
        if s + 1 < nsub:
            order += [(s + 1, d) for d in range(half)]
        order += [(s, d) for d in range(half, nchan)]

    def pass_on(s, d):
        to_across(s, d).wait_recv()
        relay(s, d).start()

    def share(s, i, count):
        units = chosen * sizes[s]
        compute(s, i * units // count, (i + 1) * units // count)

    lag = half
    skip = half // 4
    for step, (s, d) in enumerate(order):
        if d:
            to_bins(s, d).wait_recv()
        if step:
            to_across(s, d).start()
            to_beside(s, d).start()
        if step == 1:
            if nsub > 2:
                whiten(2)
                send_part(2, near)
            if nsub > 1:
                send_part(1, far)
        if d == half and s + 3 < nsub:
            whiten(s + 3)
            send_part(s + 3, near)
        if d >= half and s + 2 < nsub:
            send_one(s + 2, nchan - 1 - (d - half))
        if step >= lag:
            pass_on(*order[step - lag])
        if step == nchan - 1:
            weights()
        if 0 < s < nsub - 1 and d >= half + skip:
            if d == half + skip:
                settle(s - 1)
            share(s - 1, d - half - skip, half - skip)
    for i, (s, d) in enumerate(order[-lag:]):
        pass_on(s, d)
        if nsub > 1:
            if i == 0:
                settle(nsub - 2)
            share(nsub - 2, i, lag)
    settle(nsub - 1)
    share(nsub - 1, 0, 1)

    for d in range(1, groups):
        tallies(d).wait_send()
    for s in range(nsub):
        for d in range(nchan):
            if d:
                to_bins(s, d).wait_send()
            to_across(s, d).wait_send()
            to_beside(s, d).wait_send()
            relay(s, d).wait_send()


def per_device(nchan, groups, spectra, counts, partner):
    _, total_bins, windows, parts, width = spectra.shape
    rounds, nblocks = partner.shape
    bins = total_bins // nchan
    chosen = nblocks // groups
    unit = bins // 16
    sizes = (4 * unit, 4 * unit, 4 * unit, 3 * unit, unit) if bins % 16 == 0 else (1,) * bins
    nsub = len(sizes)
    cfg = (nchan, groups, sizes, chosen, rounds, windows, width)
    x = spectra.reshape(total_bins, windows * parts, width)
    dma = pltpu.SemaphoreType.DMA
    flops = 2 * chosen * rounds * bins * width * (2 * width) * (2 * groups * windows)
    return pl.pallas_call(
        functools.partial(kernel, cfg),
        out_shape=jax.ShapeDtypeStruct((chosen, rounds, bins, width, 2 * width), jnp.bfloat16),
        in_specs=[
            pl.BlockSpec(memory_space=pltpu.VMEM),
            pl.BlockSpec(memory_space=pltpu.VMEM),
            pl.BlockSpec(memory_space=pltpu.SMEM),
        ],
        out_specs=pl.BlockSpec(memory_space=pltpu.VMEM),
        scratch_shapes=[
            pltpu.VMEM((groups, nblocks, LANES), jnp.float32),
            pltpu.VMEM((max(sizes), 2 * windows, width), jnp.float32),
            pltpu.VMEM((nblocks, LANES), jnp.float32),
            pltpu.VMEM((chosen, rounds, groups * windows, width), jnp.bfloat16),
            pltpu.VMEM((chosen, rounds, 8, width), jnp.float32),
        ]
        + [dma((nsub, nchan))] * 8
        + [dma((groups,))] * 2
        + [pltpu.VMEM((nblocks, groups, size, 2 * windows, width), jnp.bfloat16) for size in sizes]
        + [pltpu.VMEM((nchan, size, 2 * windows, width), jnp.bfloat16) for size in sizes],
        compiler_params=pltpu.CompilerParams(
            collective_id=0, has_side_effects=True, vmem_limit_bytes=40 * 1024 * 1024),
        cost_estimate=pl.CostEstimate(flops=flops, bytes_accessed=8 << 20, transcendentals=0),
    )(x, counts.T, partner)


def solution(mesh):
    sizes = dict(mesh.shape)
    placed = (P("chan", None, "win", None, None), P("win", None), P())
    return jax.shard_map(
        functools.partial(per_device, sizes["chan"], sizes["win"]),
        mesh=mesh,
        in_specs=placed,
        out_specs=P("win", None, "chan", None, None),
        check_vma=False,
    )
```

```python
import functools

import jax
import jax.numpy as jnp
from jax import lax
from jax.experimental import pallas as pl
from jax.experimental.pallas import tpu as pltpu
from jax.sharding import PartitionSpec as P

NSAMP = 256
EPS = 1e-06
LANES = 128
MESH = pl.DeviceIdType.MESH


def flip(index, bits):
    out, place = index, 1
    while place <= bits:
        if bits & place:
            out = out + place * (1 - 2 * ((index // place) % 2))
        place *= 2
    return out


def kernel(cfg, x_ref, counts_ref, partner_ref, out_ref, *scratch):
    nchan, groups, sizes, chosen, rounds, windows, width = cfg
    (tall, raw, cts, wgt, inv, sem_as, sem_ar, sem_ys, sem_yr, sem_bs, sem_br,
     sem_cs, sem_cr, sem_ts, sem_tr) = scratch[:15]
    nsub, bins = len(sizes), sum(sizes)
    starts = [sum(sizes[:s]) for s in range(nsub)]
    held, send = scratch[15:15 + nsub], scratch[15 + nsub:]
    total_bins = nchan * bins
    me = lax.axis_index("chan")
    mine = lax.axis_index("win")
    across, beside = flip(mine, 2), flip(mine, 1)
    rows = 2 * windows

    barrier = pltpu.get_barrier_semaphore()
    for d in range(1, nchan):
        pl.semaphore_signal(barrier, 1, device_id={"chan": flip(me, d)}, device_id_type=MESH)
    for d in range(1, groups):
        pl.semaphore_signal(barrier, 1, device_id={"win": flip(mine, d)}, device_id_type=MESH)

    def to_bins(s, d, peer=None):
        peer = flip(me, d) if peer is None else peer
        return pltpu.make_async_remote_copy(
            src_ref=send[s].at[peer], dst_ref=held[s].at[me, mine],
            send_sem=sem_as.at[s, d], recv_sem=sem_ar.at[s, d],
            device_id={"chan": peer}, device_id_type=MESH)

    half, quarter = nchan // 2, nchan // 4
    inner = ((me // half) + (me // quarter)) % 2

    def send_one(s, d):
        peer = flip(me, d)
        if d >= half:
            peer = peer + inner * quarter * (1 - 2 * ((peer // quarter) % 2))
            d = d + inner * quarter * (1 - 2 * ((d // quarter) % 2))
        to_bins(s, d, peer).start()

    near, far = range(1, half), range(nchan - 1, half - 1, -1)

    def send_part(s, part):
        for d in part:
            send_one(s, d)

    def to_across(s, d):
        block = held[s].at[flip(me, d), mine]
        return pltpu.make_async_remote_copy(
            src_ref=block, dst_ref=block, send_sem=sem_ys.at[s, d], recv_sem=sem_yr.at[s, d],
            device_id={"win": across}, device_id_type=MESH)

    def to_beside(s, d):
        block = held[s].at[flip(me, d), mine]
        return pltpu.make_async_remote_copy(
            src_ref=block, dst_ref=block, send_sem=sem_bs.at[s, d], recv_sem=sem_br.at[s, d],
            device_id={"win": beside}, device_id_type=MESH)

    def relay(s, d):
        block = held[s].at[flip(me, d), across]
        return pltpu.make_async_remote_copy(
            src_ref=block, dst_ref=block, send_sem=sem_cs.at[s, d], recv_sem=sem_cr.at[s, d],
            device_id={"win": beside}, device_id_type=MESH)

    def tallies(d):
        return pltpu.make_async_remote_copy(
            src_ref=tall.at[mine], dst_ref=tall.at[mine],
            send_sem=sem_ts.at[d], recv_sem=sem_tr.at[d],
            device_id={"win": flip(mine, d)}, device_id_type=MESH)

    def add_power(f, acc):
        v = x_ref[f].astype(jnp.float32)
        return acc + v * v

    acc = lax.fori_loop(0, total_bins, add_power, jnp.zeros((rows, width), jnp.float32), unroll=4)
    raw[0] = acc
    power = (raw[0, pl.ds(0, windows, stride=2), :] + raw[0, pl.ds(1, windows, stride=2), :]) * (1.0 / total_bins)
    scale = lax.rsqrt(power + EPS)

    def whiten(s):
        def one(j, carry):
            for q in range(sizes[s]):
                raw[q] = x_ref[j * bins + starts[s] + q].astype(jnp.float32)
            for q in range(sizes[s]):
                for k in range(2):
                    part = raw[q, pl.ds(k, windows, stride=2), :] * scale
                    send[s][j, q, pl.ds(k * windows, windows), :] = part.astype(jnp.bfloat16)
            return carry

        lax.fori_loop(0, nchan, one, 0)
        held[s][me, mine] = send[s][me]

    tall[mine] = jnp.zeros(tall.shape[1:], jnp.float32)
    tall[mine, :, pl.ds(0, windows)] = counts_ref[...].astype(jnp.float32)

    whiten(0)
    pl.semaphore_wait(barrier, nchan - 1 + groups - 1)
    to_across(0, 0).start()
    to_beside(0, 0).start()
    send_part(0, near)
    for d in range(1, groups):
        tallies(d).start()
    if nsub > 1:
        whiten(1)
        send_part(1, near)
    send_part(0, far)

    def weights():
        for d in range(1, groups):
            tallies(d).wait_recv()
        whole = tall[0]
        for g in range(1, groups):
            whole = whole + pltpu.roll(tall[g], g * windows, 1)
        cts[...] = whole
        first = mine * chosen

        def one(n, carry):
            own = cts[pl.ds(first + n, 1), :]
            for r in range(rounds):
                row = jnp.minimum(own, cts[pl.ds(partner_ref[r, first + n], 1), :]) * (1.0 / NSAMP)
                wgt[n, r] = jnp.broadcast_to(row, (LANES, LANES)).T.astype(jnp.bfloat16)
                norm = lax.rsqrt(jnp.sum(row * row, axis=1, keepdims=True))
                inv[n, r] = jnp.broadcast_to(norm, (8, width))
            return carry

        lax.fori_loop(0, chosen, one, 0)

    def planes(s, block, q):
        return [
            jnp.concatenate(
                [held[s][block, g, q, pl.ds(k * windows, windows), :] for g in range(groups)], axis=0)
            for k in range(2)
        ]

    def unit(s, u):
        n, q = u // sizes[s], u % sizes[s]
        a = mine * chosen + n
        re, im = planes(s, a, q)
        re, im = re.T, im.T
        lhs = jnp.concatenate(
            [jnp.concatenate([re, im], axis=1), jnp.concatenate([im, -re], axis=1)], axis=0)
        mates = []
        for r in range(rounds):
            w = wgt[n, r]
            mre, mim = planes(s, partner_ref[r, a], q)
            mates.append(jnp.concatenate([mre * w, mim * w], axis=0))
        rhs = jnp.concatenate(mates, axis=1)
        res = jnp.dot(lhs, rhs, preferred_element_type=jnp.float32)
        for r in range(rounds):
            norm = inv[n, r, pl.ds(0, 1), :]
            for k in range(2):
                tile = res[k * width:(k + 1) * width, r * width:(r + 1) * width] * norm
                out_ref[n, r, starts[s] + q, :, pl.ds(k * width, width)] = tile.astype(jnp.bfloat16)

    def compute(s, low, high):
        lax.fori_loop(low, high, lambda u, carry: (unit(s, u), carry)[1], 0, unroll=2 if (high - low) % 2 == 0 else 1)

    def settle(s):
        for d in range(nchan):
            to_beside(s, d).wait_recv()
            relay(s, d).wait_recv()

    order = [(0, d) for d in range(half)]
    for s in range(nsub):
        if s + 1 < nsub:
            order += [(s + 1, d) for d in range(half)]
        order += [(s, d) for d in range(half, nchan)]

    def pass_on(s, d):
        to_across(s, d).wait_recv()
        relay(s, d).start()

    def share(s, i, count):
        units = chosen * sizes[s]
        compute(s, i * units // count, (i + 1) * units // count)

    lag = half
    skip = half // 4
    for step, (s, d) in enumerate(order):
        if d:
            to_bins(s, d).wait_recv()
        if step:
            to_across(s, d).start()
            to_beside(s, d).start()
        if step == 1:
            if nsub > 2:
                whiten(2)
                send_part(2, near)
            if nsub > 1:
                send_part(1, far)
        if d == half and s + 3 < nsub:
            whiten(s + 3)
            send_part(s + 3, near)
        if d >= half and s + 2 < nsub:
            send_one(s + 2, nchan - 1 - (d - half))
        if step >= lag:
            pass_on(*order[step - lag])
        if step == nchan - 1:
            weights()
        if 0 < s < nsub - 1 and d >= half + skip:
            if d == half + skip:
                settle(s - 1)
            share(s - 1, d - half - skip, half - skip)
    for i, (s, d) in enumerate(order[-lag:]):
        pass_on(s, d)
        if nsub > 1:
            if i == 0:
                settle(nsub - 2)
            share(nsub - 2, i, lag)
    settle(nsub - 1)
    share(nsub - 1, 0, 1)

    for d in range(1, groups):
        tallies(d).wait_send()
    for s in range(nsub):
        for d in range(nchan):
            if d:
                to_bins(s, d).wait_send()
            to_across(s, d).wait_send()
            to_beside(s, d).wait_send()
            relay(s, d).wait_send()


def per_device(nchan, groups, spectra, counts, partner):
    _, total_bins, windows, parts, width = spectra.shape
    rounds, nblocks = partner.shape
    bins = total_bins // nchan
    chosen = nblocks // groups
    unit = bins // 8
    sizes = (unit, 2 * unit, 2 * unit, unit, unit, unit) if bins % 8 == 0 else (1,) * bins
    nsub = len(sizes)
    cfg = (nchan, groups, sizes, chosen, rounds, windows, width)
    x = spectra.reshape(total_bins, windows * parts, width)
    dma = pltpu.SemaphoreType.DMA
    flops = 2 * chosen * rounds * bins * width * (2 * width) * (2 * groups * windows)
    return pl.pallas_call(
        functools.partial(kernel, cfg),
        out_shape=jax.ShapeDtypeStruct((chosen, rounds, bins, width, 2 * width), jnp.bfloat16),
        in_specs=[
            pl.BlockSpec(memory_space=pltpu.VMEM),
            pl.BlockSpec(memory_space=pltpu.VMEM),
            pl.BlockSpec(memory_space=pltpu.SMEM),
        ],
        out_specs=pl.BlockSpec(memory_space=pltpu.VMEM),
        scratch_shapes=[
            pltpu.VMEM((groups, nblocks, LANES), jnp.float32),
            pltpu.VMEM((max(sizes), 2 * windows, width), jnp.float32),
            pltpu.VMEM((nblocks, LANES), jnp.float32),
            pltpu.VMEM((chosen, rounds, groups * windows, width), jnp.bfloat16),
            pltpu.VMEM((chosen, rounds, 8, width), jnp.float32),
        ]
        + [dma((nsub, nchan))] * 8
        + [dma((groups,))] * 2
        + [pltpu.VMEM((nblocks, groups, size, 2 * windows, width), jnp.bfloat16) for size in sizes]
        + [pltpu.VMEM((nchan, size, 2 * windows, width), jnp.bfloat16) for size in sizes],
        compiler_params=pltpu.CompilerParams(
            collective_id=0, has_side_effects=True, vmem_limit_bytes=40 * 1024 * 1024),
        cost_estimate=pl.CostEstimate(flops=flops, bytes_accessed=8 << 20, transcendentals=0),
    )(x, counts.T, partner)


def solution(mesh):
    sizes = dict(mesh.shape)
    placed = (P("chan", None, "win", None, None), P("win", None), P())
    return jax.shard_map(
        functools.partial(per_device, sizes["chan"], sizes["win"]),
        mesh=mesh,
        in_specs=placed,
        out_specs=P("win", None, "chan", None, None),
        check_vma=False,
    )
```
